32 devices in a mesh: segment: 4 (over z), chan: 4 (over y, core), dp: 2 (over x).
Axes of the slice: x: 2, y: 2, z: 4, core: 2. Of those that a mesh axis runs over, the one named last changes fastest.
Arguments:
- grad_top: bfloat16 [2, 1536, 256], P('dp', None, 'chan'), may hold values from -6 to 6
- inputs_one: bfloat16 [4, 2, 1536, 256], P('segment', 'dp', 'chan'), may hold values from -6 to 6
- conv_one: bfloat16 [4, 2, 1536, 256], P('segment', 'dp', 'chan'), may hold values from -130 to 130
- inputs_two: bfloat16 [4, 2, 1536, 256], P('segment', 'dp', 'chan'), may hold values from -6 to 6
- conv_two: bfloat16 [4, 2, 1536, 256], P('segment', 'dp', 'chan'), may hold values from -130 to 130
- proj_weight: bfloat16 [4, 2, 1536, 1536], P('segment', None, 'chan'), may hold values from -0.15625 to 0.15625
- conv_weight: bfloat16 [4, 2, 1536, 432], P('segment', None, 'chan'), may hold values from -0.3125 to 0.3125
- norm_gain: float32 [4, 2, 1536], P('segment', None, 'chan'), may hold values from 0.1 to 1.9
- norm_bias: float32 [4, 2, 1536], P('segment', None, 'chan'), may hold values from -4 to 4
Outputs:
- grad_latent: bfloat16 [4, 2, 1536, 256], P('segment', 'dp', None, 'chan')
- grad_proj: float32 [4, 2, 1536, 1536], P('segment', None, 'chan')
- grad_conv: float32 [4, 2, 1536, 432], P('segment', None, 'chan')
- grad_gain: float32 [4, 2, 1536], P('segment', None, 'chan')
- grad_bias: float32 [4, 2, 1536], P('segment', None, 'chan')
The draws below stay inside these ranges and needn't reach their ends.
All inputs are finite; a program needn't handle non-finite values.
Results may differ from the reference program's by a relative error of at most 0.009.
Values may be sent and summed in bfloat16 or wider, within the bound.
A program may use at most 64 MiB of HBM per device.

```python
import math
import jax
import jax.numpy as jnp
from jax import lax

C = 1536
GS = 48
WW = 64
ROWS = 4
SEGMENTS = 4
MBS = 2
P_SIZE = 256


def pre_norm_draw(key):
    first_key, second_key, third_key, fourth_key = jax.random.split(key, 4)
    chan_scale = jnp.exp(jax.random.uniform(second_key, (SEGMENTS, MBS, C, 1), jnp.float32) * math.log(10.0))
    pos_scale = jnp.exp(jax.random.uniform(third_key, (SEGMENTS, MBS, 1, P_SIZE), jnp.float32) * math.log(10.0))
    base = jnp.clip(jax.random.normal(first_key, (SEGMENTS, MBS, C, P_SIZE), jnp.float32), -4.0, 4.0)
    offset = jnp.clip(jax.random.normal(fourth_key, (SEGMENTS, MBS, C, 1), jnp.float32), -3.0, 3.0)
    return (base * chan_scale * pos_scale * 0.3 + offset).astype(jnp.bfloat16)


def draw_conv_one(key, part):
    return pre_norm_draw(jax.random.fold_in(key, 11))


def draw_conv_two(key, part):
    return pre_norm_draw(jax.random.fold_in(key, 12))


def shard_levels(rng, dims, cuts, low, high):
    def one(position, blocks):
        heights = jax.random.uniform(jax.random.fold_in(jax.random.fold_in(rng, 6), position), (blocks,), jnp.float32, low / len(cuts), high / len(cuts))
        return jnp.repeat(jnp.exp(heights), dims[position] // blocks).reshape((-1,) + (1,) * (len(dims) - position - 1))

    level = one(*cuts[0])
    for cut in cuts[1:]:
        level = level * one(*cut)
    return level


def gaussian(stream_key, shape, deviation, reach, cuts=(), dtype=jnp.bfloat16):
    drawn = jax.random.normal(stream_key, shape, jnp.float32) * deviation
    if len(cuts) > 0:
        drawn = shard_levels(stream_key, shape, cuts, -0.22, 0.18) * drawn
    return jnp.clip(drawn, min=-reach, max=reach).astype(dtype)


def setup_inputs(seed: int = 0) -> dict:
    seeds = jax.random.split(jax.random.key(seed), 10)
    grad_top = gaussian(seeds[0], (MBS, C, P_SIZE), 1.0, 6.0, ((0, 2), (2, 4)))
    inputs_one = gaussian(seeds[1], (SEGMENTS, MBS, C, P_SIZE), 1.0, 6.0, ((0, 4), (1, 2), (2, 4)))
    conv_one = draw_conv_one(jax.random.fold_in(seeds[9], 71), 0)
    inputs_two = gaussian(seeds[3], (SEGMENTS, MBS, C, P_SIZE), 1.0, 6.0, ((0, 4), (1, 2), (2, 4)))
    conv_two = draw_conv_two(jax.random.fold_in(seeds[9], 71), 0)
    proj_weight = gaussian(seeds[5], (SEGMENTS, 2, C, C), C ** -0.5, 0.15625, ((0, 4), (2, 4)))
    conv_weight = gaussian(seeds[6], (SEGMENTS, 2, C, 9 * GS), (9 * GS) ** -0.5, 0.3125, ((0, 4), (2, 4)))
    norm_gain = jnp.clip(1.0 + 0.18 * jax.random.normal(seeds[7], (SEGMENTS, 2, C), jnp.float32), 0.1, 1.9)
    norm_bias = gaussian(seeds[8], (SEGMENTS, 2, C), 1.0, 4.0, ((0, 4), (2, 4)), jnp.float32)
    return {"grad_top": grad_top, "inputs_one": inputs_one, "conv_one": conv_one, "inputs_two": inputs_two, "conv_two": conv_two, "proj_weight": proj_weight, "conv_weight": conv_weight, "norm_gain": norm_gain, "norm_bias": norm_bias}


NORM_EPS = 1e-05

def tap_shift(values, step_row, step_col):
    leading = values.shape[:2]
    grid_view = values.reshape(leading + (ROWS, WW))
    padded = jnp.pad(grid_view, ((0, 0), (0, 0), (1, 1), (1, 1)))
    window = padded[:, :, 1 + step_row:1 + step_row + ROWS, 1 + step_col:1 + step_col + WW]
    return window.reshape(leading + (ROWS * WW,))

def block_back(grad_in, saved_in, saved_pre, w_proj, w_conv, gain_vec, bias_vec):
    chans, positions = saved_pre.shape
    groups_here = chans // GS
    pre = saved_pre.astype(jnp.float32).reshape(groups_here, GS, positions)
    centre = lax.optimization_barrier(jnp.mean(pre, axis=(1, 2), keepdims=True))
    varied = lax.optimization_barrier(jnp.mean(jnp.square(pre - centre), axis=(1, 2), keepdims=True))
    inv_std = 1.0 / jnp.sqrt(varied + NORM_EPS)
    normed = (pre - centre) * inv_std
    gain_grid = gain_vec.reshape(groups_here, GS, 1)
    scaled = normed * gain_grid + bias_vec.reshape(groups_here, GS, 1)
    gate_vals = jax.nn.sigmoid(scaled)
    act_bf = (scaled * gate_vals).astype(jnp.bfloat16).reshape(chans, positions)
    grad_act = jnp.dot(w_proj, grad_in, preferred_element_type=jnp.float32).reshape(groups_here, GS, positions)
    proj_grad = jnp.dot(act_bf, grad_in.T, preferred_element_type=jnp.float32)
    grad_norm = grad_act * (gate_vals * (1.0 + scaled * (1.0 - gate_vals)))
    gain_grad = lax.optimization_barrier(jnp.sum(grad_norm * normed, axis=2)).reshape(chans)
    bias_grad = lax.optimization_barrier(jnp.sum(grad_norm, axis=2)).reshape(chans)
    weighted = grad_norm * gain_grid
    first_mean = lax.optimization_barrier(jnp.mean(weighted, axis=(1, 2), keepdims=True))
    second_mean = lax.optimization_barrier(jnp.mean(weighted * normed, axis=(1, 2), keepdims=True))
    grad_pre = (inv_std * (weighted - first_mean - normed * second_mean)).astype(jnp.bfloat16)
    saved_grid = saved_in.reshape(groups_here, GS, positions).astype(jnp.float32)
    grad_wide = grad_pre.astype(jnp.float32)
    taps_w = w_conv.astype(jnp.float32).reshape(groups_here, GS, 9, GS)
    conv_parts = []
    back_sum = jnp.zeros((groups_here, GS, positions), jnp.float32)
    for tap_row in (-1, 0, 1):
        for tap_col in (-1, 0, 1):
            tap_at = 3 * (tap_row + 1) + tap_col + 1
            source = tap_shift(saved_grid, tap_row, tap_col)
            conv_parts.append(jnp.einsum('gop,gjp->goj', grad_wide, source, precision=lax.Precision.HIGHEST))
            spread_back = jnp.einsum('goj,gop->gjp', taps_w[:, :, tap_at, :], grad_wide, precision=lax.Precision.HIGHEST)
            back_sum = back_sum + tap_shift(spread_back, -tap_row, -tap_col)
    conv_grad = jnp.stack(conv_parts, axis=2).reshape(chans, 9 * GS)
    branch = back_sum.reshape(chans, positions).astype(jnp.bfloat16)
    out_grad = (grad_in.astype(jnp.float32) + branch.astype(jnp.float32)).astype(jnp.bfloat16)
    return (out_grad, (proj_grad, conv_grad, gain_grad, bias_grad))

def section_back(entering, ins_one, pre_one, ins_two, pre_two, w_proj, w_conv, gains, biases):

    def one_micro(running, micro_items):
        grad_in, x_one, h_one, x_two, h_two = micro_items
        mid_grad, grads_two = block_back(grad_in, x_two, h_two, w_proj[1], w_conv[1], gains[1], biases[1])
        out_grad, grads_one = block_back(mid_grad, x_one, h_one, w_proj[0], w_conv[0], gains[0], biases[0])
        updated = tuple((acc + jnp.stack((first_part, second_part)) for acc, first_part, second_part in zip(running, grads_one, grads_two)))
        return (updated, out_grad)
    initial = (jnp.zeros((2, C, C), jnp.float32), jnp.zeros((2, C, 9 * GS), jnp.float32), jnp.zeros((2, C), jnp.float32), jnp.zeros((2, C), jnp.float32))
    return lax.scan(one_micro, initial, (entering, ins_one, pre_one, ins_two, pre_two))

def reference(grad_top, inputs_one, conv_one, inputs_two, conv_two, proj_weight, conv_weight, norm_gain, norm_bias):
    entering = grad_top
    latents, projs, convs, gains_out, biases_out = ([], [], [], [], [])
    for segment_at in range(SEGMENTS - 1, -1, -1):
        sums_here, grads_here = section_back(entering, inputs_one[segment_at], conv_one[segment_at], inputs_two[segment_at], conv_two[segment_at], proj_weight[segment_at], conv_weight[segment_at], norm_gain[segment_at], norm_bias[segment_at])
        latents.insert(0, grads_here)
        projs.insert(0, sums_here[0])
        convs.insert(0, sums_here[1])
        gains_out.insert(0, sums_here[2])
        biases_out.insert(0, sums_here[3])
        entering = grads_here
    return (jnp.stack(latents), jnp.stack(projs), jnp.stack(convs), jnp.stack(gains_out), jnp.stack(biases_out))
```

```python
import functools

import jax
import jax.numpy as jnp
from jax import lax
from jax.experimental import pallas as pl
from jax.experimental.pallas import tpu as pltpu
from jax.sharding import PartitionSpec as P

GS = 48
WW = 64
NORM_EPS = 1e-05
MESH = pl.DeviceIdType.MESH


def norm_forward(pre_t, gain, bias):
    positions, chans = pre_t.shape
    groups = chans // GS
    grid = pre_t.reshape(positions, groups, GS)
    centre = jnp.mean(grid, axis=(0, 2), keepdims=True)
    varied = jnp.mean(jnp.square(grid - centre), axis=(0, 2), keepdims=True)
    spread = lambda v: jnp.broadcast_to(v, (1, groups, GS)).reshape(1, chans)
    inv_std = spread(lax.rsqrt(varied + NORM_EPS))
    normed = (pre_t - spread(centre)) * inv_std
    scaled = normed * gain[None] + bias[None]
    gate = jax.nn.sigmoid(scaled)
    act = (scaled * gate).astype(jnp.bfloat16)
    slope = gate * (1.0 + scaled * (1.0 - gate))
    return normed, slope, inv_std, act


def chain_kernel(
    segments, n_chan, micro, gtop, wproj, wconv, gmat, slope, normed, gain, inv_std,
    ga_buf, gb_buf, gh_out, last_out, sums_out, taps,
    send_sems, recv_sems, relay_send, relay_recv,
):
    seg = lax.axis_index("segment")
    me = lax.axis_index("chan")
    pos, width = gh_out.shape[2:]
    chips = n_chan // 2
    core = lax.rem(me, 2)
    row = me // 2
    sibling = row * 2 + 1 - core
    peers = [lax.rem(row + d, chips) * 2 + core for d in range(1, chips)]

    barrier = pltpu.get_barrier_semaphore()
    for other in [sibling] + peers:
        pl.semaphore_signal(barrier, inc=1, device_id={"chan": other}, device_id_type=MESH)

    @pl.when(seg > 0)
    def _():
        pl.semaphore_signal(barrier, inc=1, device_id={"segment": seg - 1}, device_id_type=MESH)

    @pl.when(seg < segments - 1)
    def _():
        pl.semaphore_signal(barrier, inc=1, device_id={"segment": seg + 1}, device_id_type=MESH)

    linked = jnp.where(seg > 0, 1, 0) + jnp.where(seg < segments - 1, 1, 0)
    pl.semaphore_wait(barrier, chips + linked)

    taps[...] = jnp.zeros_like(taps)

    def push(buf, which, slot, piece, target):
        return pltpu.make_async_remote_copy(
            src_ref=buf.at[piece],
            dst_ref=buf.at[piece],
            send_sem=send_sems.at[which, slot],
            recv_sem=recv_sems.at[which, piece],
            device_id={"chan": target},
            device_id_type=MESH,
        )

    def gather(buf, which):
        started = [push(buf, which, 1 + d, me, peer) for d, peer in enumerate(peers)]
        started.append(push(buf, which, 0, me, sibling))
        for copy in started:
            copy.start()
        for d, peer in enumerate(peers):
            push(buf, which, 1 + d, peer, peer).wait_recv()
            hop = push(buf, which, chips + d, peer, sibling)
            hop.start()
            started.append(hop)
        push(buf, which, 0, sibling, sibling).wait_recv()
        for d in range(1, chips):
            piece = lax.rem(row + d, chips) * 2 + 1 - core
            push(buf, which, 0, piece, sibling).wait_recv()
        for copy in started:
            copy.wait_send()

    def relay(m):
        return pltpu.make_async_remote_copy(
            src_ref=last_out.at[m],
            dst_ref=ga_buf.at[m, me],
            send_sem=relay_send.at[m],
            recv_sem=relay_recv.at[m],
            device_id={"segment": lax.rem(seg + segments - 1, segments)},
            device_id_type=MESH,
        )

    column = lax.rem(lax.broadcasted_iota(jnp.int32, (pos, width), 0), WW)

    def block(m, b, buf):
        acc = jnp.zeros((pos, width), jnp.float32)
        for piece in range(n_chan):
            acc = acc + lax.dot_general(
                buf[piece], wproj[b, piece], (((1,), (1,)), ((), ())),
                preferred_element_type=jnp.float32,
            )
        xhat = normed[m, b]
        gn = acc * slope[m, b]
        bias_row = jnp.sum(gn, axis=0, keepdims=True)
        gain_row = jnp.sum(gn * xhat, axis=0, keepdims=True)
        sums_out[m, b, 0:1] = gain_row
        sums_out[m, b, 1:2] = bias_row
        gains = gain[b]
        lane = lax.broadcasted_iota(jnp.int32, (8, width), 0)
        pair = jnp.where(lane == 0, bias_row * gains, jnp.where(lane == 1, gain_row * gains, 0.0))
        means = jnp.dot(
            pair, gmat[...], precision=lax.Precision.HIGHEST, preferred_element_type=jnp.float32
        ) * (1.0 / (GS * pos))
        gh = inv_std[m, b] * (gn * gains - means[0:1] - xhat * means[1:2])
        gh = gh.astype(jnp.bfloat16)
        gh_out[m, b] = gh
        wide = gh.astype(jnp.float32)
        taps[0, WW:WW + pos] = jnp.where(
            column == WW - 1, 0.0, pltpu.roll(wide, pos - 1, 0)
        ).astype(jnp.bfloat16)
        taps[1, WW:WW + pos] = gh
        taps[2, WW:WW + pos] = jnp.where(
            column == 0, 0.0, pltpu.roll(wide, 1, 0)
        ).astype(jnp.bfloat16)
        back = jnp.zeros((pos, width), jnp.float32)
        for dr in range(3):
            start = WW - WW * (dr - 1)
            for dc in range(3):
                back = back + jnp.dot(
                    taps[dc, start:start + pos], wconv[b, 3 * dr + dc],
                    preferred_element_type=jnp.float32,
                )
        branch = back.astype(jnp.bfloat16).astype(jnp.float32)
        return (buf[me].astype(jnp.float32) + branch).astype(jnp.bfloat16)

    for m in range(micro):
        @pl.when(seg == segments - 1)
        def _():
            ga_buf[m] = gtop[m]

        @pl.when(seg < segments - 1)
        def _():
            relay(m).wait_recv()
            gather(ga_buf.at[m], 2 * m)

        gb_buf[m, me] = block(m, 1, ga_buf.at[m])
        gather(gb_buf.at[m], 2 * m + 1)
        last_out[m] = block(m, 0, gb_buf.at[m])

        @pl.when(seg > 0)
        def _():
            relay(m).start()

    for m in range(micro):
        @pl.when(seg > 0)
        def _():
            relay(m).wait_send()


def shifted(values, step_row, step_col):
    length = values.shape[-1]
    margin = WW + 1
    padded = jnp.pad(values, ((0, 0),) * (values.ndim - 1) + ((margin, margin),))
    start = margin + step_row * WW + step_col
    view = lax.slice_in_dim(padded, start, start + length, axis=values.ndim - 1)
    column = jnp.arange(length, dtype=jnp.int32) % WW
    inside = (column + step_col >= 0) & (column + step_col < WW)
    return jnp.where(inside, view, jnp.zeros((), values.dtype))


def per_device(
    segments, n_chan,
    grad_top, inputs_one, conv_one, inputs_two, conv_two,
    proj_weight, conv_weight, norm_gain, norm_bias,
):
    micro = grad_top.shape[0]
    width, pos = conv_one.shape[2:]
    groups = width // GS
    chans = proj_weight.shape[3]
    bf = jnp.bfloat16
    f32 = jnp.float32

    top = lax.all_gather(jnp.swapaxes(grad_top, 1, 2), "chan", axis=1, tiled=True)
    top = top.reshape(micro, pos, n_chan, width).transpose(0, 2, 1, 3)

    fwd = jax.vmap(jax.vmap(norm_forward), in_axes=(0, None, None))
    pre = jnp.stack((conv_one[0], conv_two[0]), axis=1)
    pre_t = jnp.swapaxes(pre, 2, 3).astype(f32)
    normed, slope, inv_std, act = fwd(pre_t, norm_gain[0], norm_bias[0])

    w_pieces = proj_weight[0].reshape(2, width, n_chan, width).transpose(0, 2, 1, 3)
    lane = jnp.arange(width)
    same = (lane[:, None] // GS) == (lane[None, :] // GS)
    taps_w = conv_weight[0].reshape(2, width, 9, GS).transpose(0, 2, 1, 3)
    w_diag = jnp.where(same, jnp.tile(taps_w, (1, 1, 1, groups)), jnp.zeros((), bf))

    vmem = pl.BlockSpec(memory_space=pltpu.VMEM)
    ga, gb, gh, last, sums = pl.pallas_call(
        functools.partial(chain_kernel, segments, n_chan, micro),
        out_shape=(
            jax.ShapeDtypeStruct((micro, n_chan, pos, width), bf),
            jax.ShapeDtypeStruct((micro, n_chan, pos, width), bf),
            jax.ShapeDtypeStruct((micro, 2, pos, width), bf),
            jax.ShapeDtypeStruct((micro, pos, width), bf),
            jax.ShapeDtypeStruct((micro, 2, 2, width), f32),
        ),
        in_specs=[vmem] * 8,
        out_specs=(vmem,) * 5,
        scratch_shapes=[
            pltpu.VMEM((3, pos + 2 * WW, width), bf),
            pltpu.SemaphoreType.DMA((2 * micro, n_chan)),
            pltpu.SemaphoreType.DMA((2 * micro, n_chan)),
            pltpu.SemaphoreType.DMA((micro,)),
            pltpu.SemaphoreType.DMA((micro,)),
        ],
        compiler_params=pltpu.CompilerParams(
            collective_id=0, has_side_effects=True, vmem_limit_bytes=56 * 1024 * 1024
        ),
    )(top, w_pieces, w_diag, same.astype(f32), slope, normed, norm_gain[0][:, None], inv_std)

    latent = lax.all_to_all(last, "chan", split_axis=1, concat_axis=2, tiled=True)
    latent = jnp.swapaxes(latent, 1, 2)[None]

    both = lambda v: lax.all_gather(v, "dp", axis=0, tiled=True)
    act_all = both(act)
    g_all = both(jnp.stack((gb, ga), axis=1))
    gh_all = both(gh)
    x_all = both(jnp.stack((inputs_one[0], inputs_two[0]), axis=1))
    n_all = act_all.shape[0]

    proj = jnp.einsum("mbpi,mbcpo->bico", act_all, g_all, preferred_element_type=f32)
    proj = proj.reshape(2, width, chans)
    x_grid = x_all.reshape(n_all, 2, groups, GS, pos)
    cols = jnp.stack(
        [shifted(x_grid, dr, dc) for dr in (-1, 0, 1) for dc in (-1, 0, 1)], axis=3
    ).reshape(n_all, 2, groups, 9 * GS, pos)
    gh_grid = jnp.swapaxes(gh_all, 2, 3).reshape(n_all, 2, groups, GS, pos)
    conv = jnp.einsum("mbgop,mbgkp->bgok", gh_grid, cols, preferred_element_type=f32)
    conv = conv.reshape(2, width, 9 * GS)
    sums = lax.psum(jnp.sum(sums, axis=0), "dp")
    return latent, proj[None], conv[None], sums[None, :, 0], sums[None, :, 1]


def solution(mesh):
    return jax.shard_map(
        functools.partial(per_device, mesh.shape["segment"], mesh.shape["chan"]),
        mesh=mesh,
        in_specs=(
            P("dp", None, "chan"),
            P("segment", "dp", "chan", None),
            P("segment", "dp", "chan", None),
            P("segment", "dp", "chan", None),
            P("segment", "dp", "chan", None),
            P("segment", None, "chan", None),
            P("segment", None, "chan", None),
            P("segment", None, "chan"),
            P("segment", None, "chan"),
        ),
        out_specs=(
            P("segment", "dp", None, "chan"),
            P("segment", None, "chan", None),
            P("segment", None, "chan", None),
            P("segment", None, "chan"),
            P("segment", None, "chan"),
        ),
        check_vma=False,
    )
```

```python
import functools

import jax
import jax.numpy as jnp
from jax import lax
from jax.experimental import pallas as pl
from jax.experimental.pallas import tpu as pltpu
from jax.sharding import PartitionSpec as P

GS = 48
WW = 64
NORM_EPS = 1e-05
MESH = pl.DeviceIdType.MESH


def norm_forward(pre_t, gain, bias):
    positions, chans = pre_t.shape
    groups = chans // GS
    grid = pre_t.reshape(positions, groups, GS)
    centre = jnp.mean(grid, axis=(0, 2), keepdims=True)
    varied = jnp.mean(jnp.square(grid - centre), axis=(0, 2), keepdims=True)
    spread = lambda v: jnp.broadcast_to(v, (1, groups, GS)).reshape(1, chans)
    inv_std = spread(lax.rsqrt(varied + NORM_EPS))
    normed = (pre_t - spread(centre)) * inv_std
    scaled = normed * gain[None] + bias[None]
    gate = jax.nn.sigmoid(scaled)
    act = (scaled * gate).astype(jnp.bfloat16)
    slope = gate * (1.0 + scaled * (1.0 - gate))
    return normed, slope, inv_std, act


def chain_kernel(
    segments, n_chan, n_dp, gtop, wproj, wconv, same, slope, normed, gain, inv_std, act, saved,
    latent, proj, conv, sums,
    g_all, gh_all, act_all, x_all, sums_all, last, taps, x_taps, w_diag, gh_turned, square,
    send_sems, recv_sems, relay_send, relay_recv, dp_send, dp_recv,
    far_send, far_recv, hop_send, lat_send, lat_recv,
):
    seg = lax.axis_index("segment")
    me = lax.axis_index("chan")
    dp = lax.axis_index("dp")
    pos, width = last.shape
    part = pos // n_chan
    chips = n_chan // 2
    core = lax.rem(me, 2)
    row = me // 2
    sibling = row * 2 + 1 - core
    peers = [lax.rem(row + d, chips) * 2 + core for d in range(1, chips)]
    others = [lax.rem(me + d, n_chan) for d in range(1, n_chan)]
    replicas = [lax.rem(dp + d, n_dp) for d in range(1, n_dp)]
    top_seg = seg == segments - 1

    barrier = pltpu.get_barrier_semaphore()
    for other in others:
        pl.semaphore_signal(barrier, inc=1, device_id={"chan": other}, device_id_type=MESH)
    for other in replicas:
        pl.semaphore_signal(barrier, inc=1, device_id={"dp": other}, device_id_type=MESH)

    @pl.when(seg > 0)
    def _():
        pl.semaphore_signal(barrier, inc=1, device_id={"segment": seg - 1}, device_id_type=MESH)

    @pl.when(seg < segments - 1)
    def _():
        pl.semaphore_signal(barrier, inc=1, device_id={"segment": seg + 1}, device_id_type=MESH)

    linked = jnp.where(seg > 0, 1, 0) + jnp.where(seg < segments - 1, 1, 0)
    pl.semaphore_wait(barrier, n_chan - 1 + n_dp - 1 + linked)

    def whole(buf):
        return lambda piece: buf.at[piece]

    def strip(buf):
        return lambda piece: buf.at[:, pl.ds(pl.multiple_of(piece * part, part), part)]

    def push(view, which, slot, piece, target):
        return pltpu.make_async_remote_copy(
            src_ref=view(piece),
            dst_ref=view(piece),
            send_sem=send_sems.at[which, slot],
            recv_sem=recv_sems.at[which, piece],
            device_id={"chan": target},
            device_id_type=MESH,
        )

    def gather_start(view, which):
        started = [push(view, which, 1 + d, me, peer) for d, peer in enumerate(peers)]
        started.append(push(view, which, 0, me, sibling))
        for copy in started:
            copy.start()
        return started

    def gather_finish(view, which, started):
        for d, peer in enumerate(peers):
            push(view, which, 1 + d, peer, peer).wait_recv()
            hop = push(view, which, chips + d, peer, sibling)
            hop.start()
            started.append(hop)
        push(view, which, 0, sibling, sibling).wait_recv()
        for d in range(1, chips):
            piece = lax.rem(row + d, chips) * 2 + 1 - core
            push(view, which, 0, piece, sibling).wait_recv()
        for copy in started:
            copy.wait_send()

    def relay():
        return pltpu.make_async_remote_copy(
            src_ref=last,
            dst_ref=g_all.at[1, dp, me],
            send_sem=relay_send,
            recv_sem=relay_recv,
            device_id={"segment": lax.rem(seg + segments - 1, segments)},
            device_id_type=MESH,
        )

    def swap(kind, d, src, dst):
        target = replicas[d]
        return pltpu.make_async_remote_copy(
            src_ref=src,
            dst_ref=dst,
            send_sem=dp_send.at[kind, d],
            recv_sem=dp_recv.at[kind, dp],
            device_id={"dp": target},
            device_id_type=MESH,
        )

    def swap_start(kind, src, buf):
        for d in range(n_dp - 1):
            swap(kind, d, src, buf.at[dp]).start()

    def swap_finish(kind, src, buf):
        for d, other in enumerate(replicas):
            pltpu.make_async_remote_copy(
                src_ref=src,
                dst_ref=buf.at[other],
                send_sem=dp_send.at[kind, d],
                recv_sem=dp_recv.at[kind, other],
                device_id={"dp": other},
                device_id_type=MESH,
            ).wait()

    def far(b, d, j, source, piece):
        return pltpu.make_async_remote_copy(
            src_ref=g_all.at[b, source, piece],
            dst_ref=g_all.at[b, source, piece],
            send_sem=far_send.at[b, d, j],
            recv_sem=far_recv.at[b, source, piece],
            device_id={"dp": replicas[d]},
            device_id_type=MESH,
        )

    def hop(b, d, j, source, piece):
        return pltpu.make_async_remote_copy(
            src_ref=g_all.at[b, source, piece],
            dst_ref=g_all.at[b, source, piece],
            send_sem=hop_send.at[b, d, j],
            recv_sem=far_recv.at[b, source, piece],
            device_id={"chan": sibling},
            device_id_type=MESH,
        )

    def far_start(b):
        for d in range(n_dp - 1):
            for j, piece in enumerate([me] + peers):
                far(b, d, j, dp, piece).start()

    def far_pass(b):
        for d, other in enumerate(replicas):
            for j, piece in enumerate([me] + peers):
                far(b, d, j, other, piece).wait_recv()
                hop(b, d, j, other, piece).start()

    def far_finish(b):
        for d, other in enumerate(replicas):
            for j in range(chips):
                piece = lax.rem(row + j, chips) * 2 + 1 - core
                hop(b, d, j, other, piece).wait_recv()
            for j, piece in enumerate([me] + peers):
                far(b, d, j, dp, piece).wait_send()
                hop(b, d, j, other, piece).wait_send()

    column = lax.rem(lax.broadcasted_iota(jnp.int32, (pos, width), 0), WW)

    def side_by_side(values):
        wide = values.astype(jnp.float32)
        ahead = jnp.where(column == WW - 1, 0.0, pltpu.roll(wide, pos - 1, 0))
        behind = jnp.where(column == 0, 0.0, pltpu.roll(wide, 1, 0))
        return ahead.astype(jnp.bfloat16), behind.astype(jnp.bfloat16)

    def spread_taps(b):
        along = lax.broadcasted_iota(jnp.int32, (9 * GS, width), 0)
        within = lax.rem(lax.broadcasted_iota(jnp.int32, (9 * GS, width), 1), GS)
        for k in range(9):
            pick = jnp.where(along == within + k * GS, 1.0, 0.0).astype(jnp.bfloat16)
            tiled = jnp.dot(wconv[b], pick, preferred_element_type=jnp.float32)
            w_diag[b, k] = (tiled * same[...]).astype(jnp.bfloat16)

    def spread_inputs():
        swap_finish(0, act, act_all)
        swap_finish(1, saved, x_all)
        x_taps[...] = jnp.zeros_like(x_taps)
        for d in range(n_dp):
            for b in range(2):
                values = x_all[d, b]
                ahead, behind = side_by_side(values)
                x_taps[b, d, 0, WW:WW + pos] = behind
                x_taps[b, d, 1, WW:WW + pos] = values
                x_taps[b, d, 2, WW:WW + pos] = ahead

    def piece_of(b, piece):
        if width % 128 == 0:
            return wproj[b, :, piece * width:(piece + 1) * width]
        return wproj[b, piece]

    def block(b):
        acc = jnp.zeros((pos, width), jnp.float32)
        for piece in range(n_chan):
            acc = acc + lax.dot_general(
                g_all[b, dp, piece], piece_of(b, piece), (((1,), (1,)), ((), ())),
                preferred_element_type=jnp.float32,
            )
        xhat = normed[b]
        gn = acc * slope[b]
        bias_row = jnp.sum(gn, axis=0, keepdims=True)
        gain_row = jnp.sum(gn * xhat, axis=0, keepdims=True)
        sums_all[dp, b, 0:1] = gain_row
        sums_all[dp, b, 1:2] = bias_row
        gains = gain[b]
        lane = lax.broadcasted_iota(jnp.int32, (8, width), 0)
        pair = jnp.where(lane == 0, bias_row * gains, jnp.where(lane == 1, gain_row * gains, 0.0))
        means = jnp.dot(
            pair, same[...], precision=lax.Precision.HIGHEST, preferred_element_type=jnp.float32
        ) * (1.0 / (GS * pos))
        gh = inv_std[b] * (gn * gains - means[0:1] - xhat * means[1:2])
        gh = gh.astype(jnp.bfloat16)
        gh_all[b, dp] = gh
        ahead, behind = side_by_side(gh)
        taps[0, WW:WW + pos] = ahead
        taps[1, WW:WW + pos] = gh
        taps[2, WW:WW + pos] = behind
        back = jnp.zeros((pos, width), jnp.float32)
        for dr in range(3):
            start = WW - WW * (dr - 1)
            for dc in range(3):
                back = back + jnp.dot(
                    taps[dc, start:start + pos], w_diag[b, 3 * dr + dc],
                    preferred_element_type=jnp.float32,
                )
        branch = back.astype(jnp.bfloat16).astype(jnp.float32)
        return (g_all[b, dp, me].astype(jnp.float32) + branch).astype(jnp.bfloat16)

    def proj_grad(b):
        for piece in range(n_chan):
            acc = jnp.zeros((width, width), jnp.float32)
            for d in range(n_dp):
                acc = acc + jnp.dot(
                    act_all[d, b], g_all[b, d, piece], preferred_element_type=jnp.float32
                )
            if width % 128 == 0:
                proj[b, :, piece * width:(piece + 1) * width] = acc
            else:
                proj[b, piece] = acc

    def conv_grad(b):
        for d in range(n_dp):
            gh_turned[d] = gh_all[b, d].astype(jnp.float32).T.astype(jnp.bfloat16)
        for dr in range(3):
            start = WW * dr
            for dc in range(3):
                at = (3 * dr + dc) * GS
                acc = jnp.zeros((width, width), jnp.float32)
                for d in range(n_dp):
                    acc = acc + jnp.dot(
                        gh_turned[d], x_taps[b, d, dc, start:start + pos],
                        preferred_element_type=jnp.float32,
                    )
                square[...] = acc
                for q in range(0, width, GS):
                    conv[b, q:q + GS, at:at + GS] = square[q:q + GS, q:q + GS]

    act_all[dp] = act[...]
    x_all[dp] = saved[...]
    taps[...] = jnp.zeros_like(taps)
    entering = g_all.at[1, dp]
    middle = g_all.at[0, dp]

    @pl.when(top_seg)
    def _():
        entering[:, pl.ds(pl.multiple_of(me * part, part), part)] = gtop[...]
        started = gather_start(strip(entering), 1)
        spread_taps(1)
        gather_finish(strip(entering), 1, started)
        swap_start(0, act, act_all)
        swap_start(1, saved, x_all)

    @pl.when(seg < segments - 1)
    def _():
        swap_start(0, act, act_all)
        swap_start(1, saved, x_all)
        spread_taps(1)
        spread_taps(0)
        spread_inputs()
        relay().wait_recv()
        gather_finish(whole(entering), 1, gather_start(whole(entering), 1))

    far_start(1)
    middle[me] = block(1)
    started = gather_start(whole(middle), 0)
    swap_start(2, gh_all.at[1, dp], gh_all.at[1])

    @pl.when(top_seg)
    def _():
        spread_taps(0)

    gather_finish(whole(middle), 0, started)
    far_start(0)
    last[...] = block(0)

    @pl.when(seg > 0)
    def _():
        relay().start()

    swap_start(3, gh_all.at[0, dp], gh_all.at[0])
    swap_start(4, sums_all.at[dp], sums_all)
    for d, other in enumerate(others):
        pltpu.make_async_remote_copy(
            src_ref=last.at[pl.ds(pl.multiple_of(other * part, part), part)],
            dst_ref=latent.at[me],
            send_sem=lat_send.at[d],
            recv_sem=lat_recv.at[me],
            device_id={"chan": other},
            device_id_type=MESH,
        ).start()
    latent[me] = last[pl.ds(pl.multiple_of(me * part, part), part)]

    @pl.when(top_seg)
    def _():
        spread_inputs()

    far_pass(1)
    swap_finish(2, gh_all.at[1, dp], gh_all.at[1])
    conv_grad(1)
    far_pass(0)
    far_finish(1)
    proj_grad(1)
    far_finish(0)
    proj_grad(0)
    swap_finish(3, gh_all.at[0, dp], gh_all.at[0])
    conv_grad(0)
    swap_finish(4, sums_all.at[dp], sums_all)
    total = sums_all[0]
    for d in range(1, n_dp):
        total = total + sums_all[d]
    sums[...] = total
    for d, other in enumerate(others):
        pltpu.make_async_remote_copy(
            src_ref=last.at[pl.ds(pl.multiple_of(other * part, part), part)],
            dst_ref=latent.at[other],
            send_sem=lat_send.at[d],
            recv_sem=lat_recv.at[other],
            device_id={"chan": other},
            device_id_type=MESH,
        ).wait()

    @pl.when(seg > 0)
    def _():
        relay().wait_send()


def per_device(
    segments, n_chan, n_dp,
    grad_top, inputs_one, conv_one, inputs_two, conv_two,
    proj_weight, conv_weight, norm_gain, norm_bias,
):
    width, pos = conv_one.shape[2:]
    part = pos // n_chan
    chans = proj_weight.shape[3]
    bf = jnp.bfloat16
    f32 = jnp.float32

    top = grad_top.reshape(n_chan, width, part).swapaxes(1, 2)
    pre = jnp.concatenate((conv_one[0], conv_two[0]), axis=0)
    pre_t = jnp.swapaxes(pre, 1, 2).astype(f32)
    normed, slope, inv_std, act = jax.vmap(norm_forward)(pre_t, norm_gain[0], norm_bias[0])
    act = jnp.swapaxes(act, 1, 2)
    saved = jnp.swapaxes(jnp.concatenate((inputs_one[0], inputs_two[0]), axis=0), 1, 2)
    lane = jnp.arange(width)
    same = ((lane[:, None] // GS) == (lane[None, :] // GS)).astype(f32)
    w_proj = proj_weight[0]
    proj_shape = (2, width, chans)
    if width % 128:
        w_proj = w_proj.reshape(2, width, n_chan, width).swapaxes(1, 2)
        proj_shape = (2, n_chan, width, width)

    vmem = pl.BlockSpec(memory_space=pltpu.VMEM)
    dma = pltpu.SemaphoreType.DMA
    chips = n_chan // 2
    apart = max(n_dp - 1, 1)
    latent, proj, conv, sums = pl.pallas_call(
        functools.partial(chain_kernel, segments, n_chan, n_dp),
        out_shape=(
            jax.ShapeDtypeStruct((n_chan, part, width), bf),
            jax.ShapeDtypeStruct(proj_shape, f32),
            jax.ShapeDtypeStruct((2, width, 9 * GS), f32),
            jax.ShapeDtypeStruct((2, 2, width), f32),
        ),
        in_specs=[vmem] * 10,
        out_specs=(vmem,) * 4,
        scratch_shapes=[
            pltpu.VMEM((2, n_dp, n_chan, pos, width), bf),
            pltpu.VMEM((2, n_dp, pos, width), bf),
            pltpu.VMEM((n_dp, 2, width, pos), bf),
            pltpu.VMEM((n_dp, 2, pos, width), bf),
            pltpu.VMEM((n_dp, 2, 2, width), f32),
            pltpu.VMEM((pos, width), bf),
            pltpu.VMEM((3, pos + 2 * WW, width), bf),
            pltpu.VMEM((2, n_dp, 3, pos + 2 * WW, width), bf),
            pltpu.VMEM((2, 9, width, width), bf),
            pltpu.VMEM((n_dp, width, pos), bf),
            pltpu.VMEM((width, width), f32),
            dma((2, n_chan)),
            dma((2, n_chan)),
            dma,
            dma,
            dma((5, apart)),
            dma((5, n_dp)),
            dma((2, apart, chips)),
            dma((2, n_dp, n_chan)),
            dma((2, apart, chips)),
            dma((n_chan,)),
            dma((n_chan,)),
        ],
        compiler_params=pltpu.CompilerParams(
            collective_id=0, has_side_effects=True, vmem_limit_bytes=60 * 1024 * 1024
        ),
    )(top, w_proj, conv_weight[0], same, slope, normed, norm_gain[0][:, None], inv_std, act, saved)

    latent = jnp.swapaxes(latent, 1, 2).reshape(1, 1, chans, part)
    if width % 128:
        proj = proj.swapaxes(1, 2).reshape(2, width, chans)
    return latent, proj[None], conv[None], sums[None, :, 0], sums[None, :, 1]


def solution(mesh):
    return jax.shard_map(
        functools.partial(
            per_device, mesh.shape["segment"], mesh.shape["chan"], mesh.shape["dp"]
        ),
        mesh=mesh,
        in_specs=(
            P("dp", None, "chan"),
            P("segment", "dp", "chan", None),
            P("segment", "dp", "chan", None),
            P("segment", "dp", "chan", None),
            P("segment", "dp", "chan", None),
            P("segment", None, "chan", None),
            P("segment", None, "chan", None),
            P("segment", None, "chan"),
            P("segment", None, "chan"),
        ),
        out_specs=(
            P("segment", "dp", None, "chan"),
            P("segment", None, "chan", None),
            P("segment", None, "chan", None),
            P("segment", None, "chan"),
            P("segment", None, "chan"),
        ),
        check_vma=False,
    )
```

```python
import functools

import jax
import jax.numpy as jnp
from jax import lax
from jax.experimental import pallas as pl
from jax.experimental.pallas import tpu as pltpu
from jax.sharding import PartitionSpec as P

GS = 48
WW = 64
NORM_EPS = 1e-05
MESH = pl.DeviceIdType.MESH


def chain_kernel(
    segments, n_chan, n_dp, gtop, wproj, wconv, gain, bias, pre_one, pre_two, in_one, in_two,
    latent, proj, conv, sums,
    g_all, gh_all, act_all, x_all, sums_all, last, taps, x_taps, w_diag, gh_turned, square,
    same, slope, normed, inv_std, act, saved, w_turned,
    send_sems, recv_sems, relay_send, relay_recv, dp_send, dp_recv,
    far_send, far_recv, hop_send, lat_send, lat_recv,
):
    seg = lax.axis_index("segment")
    me = lax.axis_index("chan")
    dp = lax.axis_index("dp")
    pos, width = last.shape
    half = width // 2
    part = pos // n_chan
    chips = n_chan // 2
    core = lax.rem(me, 2)
    row = me // 2
    sibling = row * 2 + 1 - core
    peers = [lax.rem(row + d, chips) * 2 + core for d in range(1, chips)]
    others = [lax.rem(me + d, n_chan) for d in range(1, n_chan)]
    replicas = [lax.rem(dp + d, n_dp) for d in range(1, n_dp)]
    top_seg = seg == segments - 1

    barrier = pltpu.get_barrier_semaphore()
    for other in others:
        pl.semaphore_signal(barrier, inc=1, device_id={"chan": other}, device_id_type=MESH)
    for other in replicas:
        pl.semaphore_signal(barrier, inc=1, device_id={"dp": other}, device_id_type=MESH)

    @pl.when(seg > 0)
    def _():
        pl.semaphore_signal(barrier, inc=1, device_id={"segment": seg - 1}, device_id_type=MESH)

    @pl.when(seg < segments - 1)
    def _():
        pl.semaphore_signal(barrier, inc=1, device_id={"segment": seg + 1}, device_id_type=MESH)

    linked = jnp.where(seg > 0, 1, 0) + jnp.where(seg < segments - 1, 1, 0)
    pl.semaphore_wait(barrier, n_chan - 1 + n_dp - 1 + linked)

    def whole(buf):
        return lambda piece: buf.at[piece]

    def strip(buf):
        return lambda piece: buf.at[:, pl.ds(pl.multiple_of(piece * part, part), part)]

    def push(view, which, slot, piece, target):
        return pltpu.make_async_remote_copy(
            src_ref=view(piece),
            dst_ref=view(piece),
            send_sem=send_sems.at[which, slot],
            recv_sem=recv_sems.at[which, piece],
            device_id={"chan": target},
            device_id_type=MESH,
        )

    def gather_start(view, which):
        started = [push(view, which, 1 + d, me, peer) for d, peer in enumerate(peers)]
        started.append(push(view, which, 0, me, sibling))
        for copy in started:
            copy.start()
        return started

    def gather_finish(view, which, started):
        for d, peer in enumerate(peers):
            push(view, which, 1 + d, peer, peer).wait_recv()
            hop = push(view, which, chips + d, peer, sibling)
            hop.start()
            started.append(hop)
        push(view, which, 0, sibling, sibling).wait_recv()
        for d in range(1, chips):
            piece = lax.rem(row + d, chips) * 2 + 1 - core
            push(view, which, 0, piece, sibling).wait_recv()
        for copy in started:
            copy.wait_send()

    def relay():
        return pltpu.make_async_remote_copy(
            src_ref=last,
            dst_ref=g_all.at[1, dp, me],
            send_sem=relay_send,
            recv_sem=relay_recv,
            device_id={"segment": lax.rem(seg + segments - 1, segments)},
            device_id_type=MESH,
        )

    def swap(kind, d, src, dst):
        target = replicas[d]
        return pltpu.make_async_remote_copy(
            src_ref=src,
            dst_ref=dst,
            send_sem=dp_send.at[kind, d],
            recv_sem=dp_recv.at[kind, dp],
            device_id={"dp": target},
            device_id_type=MESH,
        )

    def swap_start(kind, src, buf):
        for d in range(n_dp - 1):
            swap(kind, d, src, buf.at[dp]).start()

    def swap_finish(kind, src, buf):
        for d, other in enumerate(replicas):
            pltpu.make_async_remote_copy(
                src_ref=src,
                dst_ref=buf.at[other],
                send_sem=dp_send.at[kind, d],
                recv_sem=dp_recv.at[kind, other],
                device_id={"dp": other},
                device_id_type=MESH,
            ).wait()

    def far(b, d, j, source, piece):
        return pltpu.make_async_remote_copy(
            src_ref=g_all.at[b, source, piece],
            dst_ref=g_all.at[b, source, piece],
            send_sem=far_send.at[b, d, j],
            recv_sem=far_recv.at[b, source, piece],
            device_id={"dp": replicas[d]},
            device_id_type=MESH,
        )

    def hop(b, d, j, source, piece):
        return pltpu.make_async_remote_copy(
            src_ref=g_all.at[b, source, piece],
            dst_ref=g_all.at[b, source, piece],
            send_sem=hop_send.at[b, d, j],
            recv_sem=far_recv.at[b, source, piece],
            device_id={"chan": sibling},
            device_id_type=MESH,
        )

    def far_start(b):
        for d in range(n_dp - 1):
            for j, piece in enumerate([me] + peers):
                far(b, d, j, dp, piece).start()

    def far_pass(b):
        for d, other in enumerate(replicas):
            for j, piece in enumerate([me] + peers):
                far(b, d, j, other, piece).wait_recv()
                hop(b, d, j, other, piece).start()

    def far_finish(b):
        for d, other in enumerate(replicas):
            for j in range(chips):
                piece = lax.rem(row + j, chips) * 2 + 1 - core
                hop(b, d, j, other, piece).wait_recv()
            for j, piece in enumerate([me] + peers):
                far(b, d, j, dp, piece).wait_send()
                hop(b, d, j, other, piece).wait_send()

    column = lax.rem(lax.broadcasted_iota(jnp.int32, (pos, width), 0), WW)

    def side_by_side(values):
        wide = values.astype(jnp.float32)
        ahead = jnp.where(column == WW - 1, 0.0, pltpu.roll(wide, pos - 1, 0))
        behind = jnp.where(column == 0, 0.0, pltpu.roll(wide, 1, 0))
        return ahead.astype(jnp.bfloat16), behind.astype(jnp.bfloat16)

    def spread_taps(b):
        along = lax.broadcasted_iota(jnp.int32, (9 * GS, width), 0)
        within = lax.rem(lax.broadcasted_iota(jnp.int32, (9 * GS, width), 1), GS)
        for k in range(9):
            pick = jnp.where(along == within + k * GS, 1.0, 0.0).astype(jnp.bfloat16)
            tiled = jnp.dot(wconv[b], pick, preferred_element_type=jnp.float32)
            tiled = tiled * same[...]
            for h in range(2):
                side = slice(h * half, (h + 1) * half)
                w_diag[b, k, h] = tiled[side, side].astype(jnp.bfloat16)

    def group_mean(rows):
        return jnp.dot(
            rows, same[...], precision=lax.Precision.HIGHEST, preferred_element_type=jnp.float32
        ) * (1.0 / (GS * pos))

    def column_sum(values):
        return jnp.broadcast_to(jnp.sum(values, axis=0, keepdims=True), (8, width))

    def norm_forward(b):
        pre = (pre_one, pre_two)[b][...].astype(jnp.float32).T
        apart = pre - group_mean(column_sum(pre))[0:1]
        inv = lax.rsqrt(group_mean(column_sum(apart * apart))[0:1] + NORM_EPS)
        xhat = apart * inv
        n = xhat * gain[b:b + 1] + bias[b:b + 1]
        gate = jax.nn.sigmoid(n)
        inv_std[b] = inv
        normed[b] = xhat
        slope[b] = gate * (1.0 + n * (1.0 - gate))
        act[b] = (n * gate).T.astype(jnp.bfloat16)
        for piece in range(n_chan):
            w_turned[b, piece] = piece_of(b, piece).astype(jnp.float32).T.astype(jnp.bfloat16)

    def inputs_start():
        act_all[dp] = act[...]
        x_all[dp] = saved[...]
        swap_start(0, act, act_all)
        swap_start(1, saved, x_all)

    def spread_inputs():
        swap_finish(0, act, act_all)
        swap_finish(1, saved, x_all)
        x_taps[...] = jnp.zeros_like(x_taps)
        for d in range(n_dp):
            for b in range(2):
                values = x_all[d, b].astype(jnp.float32).T.astype(jnp.bfloat16)
                ahead, behind = side_by_side(values)
                x_taps[b, d, 0, WW:WW + pos] = behind
                x_taps[b, d, 1, WW:WW + pos] = values
                x_taps[b, d, 2, WW:WW + pos] = ahead

    def piece_of(b, piece):
        if width % 128 == 0:
            return wproj[b, :, piece * width:(piece + 1) * width]
        return wproj[b, piece]

    def block(b):
        acc = jnp.zeros((pos, width), jnp.float32)
        for piece in range(n_chan):
            acc = acc + lax.dot_general(
                g_all[b, dp, piece], w_turned[b, piece], (((1,), (0,)), ((), ())),
                preferred_element_type=jnp.float32,
            )
        xhat = normed[b]
        gn = acc * slope[b]
        bias_row = jnp.sum(gn, axis=0, keepdims=True)
        gain_row = jnp.sum(gn * xhat, axis=0, keepdims=True)
        sums_all[dp, b, 0:1] = gain_row
        sums_all[dp, b, 1:2] = bias_row
        gains = gain[b:b + 1]
        lane = lax.broadcasted_iota(jnp.int32, (8, width), 0)
        pair = jnp.where(lane == 0, bias_row * gains, jnp.where(lane == 1, gain_row * gains, 0.0))
        means = group_mean(pair)
        gh = inv_std[b] * (gn * gains - means[0:1] - xhat * means[1:2])
        gh = gh.astype(jnp.bfloat16)
        gh_all[b, dp] = gh
        ahead, behind = side_by_side(gh)
        sides = []
        for h in range(2):
            side = slice(h * half, (h + 1) * half)
            for dc, view in enumerate((ahead, gh, behind)):
                taps[h, dc, WW:WW + pos] = view[:, side]
            back = jnp.zeros((pos, half), jnp.float32)
            for dr in range(3):
                start = WW - WW * (dr - 1)
                for dc in range(3):
                    back = back + jnp.dot(
                        taps[h, dc, start:start + pos], w_diag[b, 3 * dr + dc, h],
                        preferred_element_type=jnp.float32,
                    )
            sides.append(back)
        back = jnp.concatenate(sides, axis=1)
        branch = back.astype(jnp.bfloat16).astype(jnp.float32)
        return (g_all[b, dp, me].astype(jnp.float32) + branch).astype(jnp.bfloat16)

    def proj_grad(b):
        for piece in range(n_chan):
            acc = jnp.zeros((width, width), jnp.float32)
            for d in range(n_dp):
                acc = acc + jnp.dot(
                    act_all[d, b], g_all[b, d, piece], preferred_element_type=jnp.float32
                )
            if width % 128 == 0:
                proj[b, :, piece * width:(piece + 1) * width] = acc
            else:
                proj[b, piece] = acc

    def conv_grad(b):
        for d in range(n_dp):
            gh_turned[d] = gh_all[b, d].astype(jnp.float32).T.astype(jnp.bfloat16)
        for dr in range(3):
            start = WW * dr
            for dc in range(3):
                at = (3 * dr + dc) * GS
                acc = jnp.zeros((width, width), jnp.float32)
                for d in range(n_dp):
                    acc = acc + jnp.dot(
                        gh_turned[d], x_taps[b, d, dc, start:start + pos],
                        preferred_element_type=jnp.float32,
                    )
                square[...] = acc
                for q in range(0, width, GS):
                    conv[b, q:q + GS, at:at + GS] = square[q:q + GS, q:q + GS]

    down = lax.broadcasted_iota(jnp.int32, (width, width), 0)
    across = lax.broadcasted_iota(jnp.int32, (width, width), 1)
    same[...] = jnp.where(lax.div(down, GS) == lax.div(across, GS), 1.0, 0.0)
    saved[0] = in_one[...]
    saved[1] = in_two[...]
    taps[...] = jnp.zeros_like(taps)
    entering = g_all.at[1, dp]
    middle = g_all.at[0, dp]

    @pl.when(top_seg)
    def _():
        entering[:, pl.ds(pl.multiple_of(me * part, part), part)] = gtop[...]
        started = gather_start(strip(entering), 1)
        norm_forward(1)
        spread_taps(1)
        gather_finish(strip(entering), 1, started)

    @pl.when(seg < segments - 1)
    def _():
        norm_forward(1)
        norm_forward(0)
        inputs_start()
        spread_taps(1)
        spread_taps(0)
        spread_inputs()
        relay().wait_recv()
        gather_finish(whole(entering), 1, gather_start(whole(entering), 1))

    far_start(1)
    middle[me] = block(1)
    started = gather_start(whole(middle), 0)
    swap_start(2, gh_all.at[1, dp], gh_all.at[1])

    @pl.when(top_seg)
    def _():
        norm_forward(0)
        spread_taps(0)
        inputs_start()

    gather_finish(whole(middle), 0, started)
    far_start(0)
    last[...] = block(0)

    @pl.when(seg > 0)
    def _():
        relay().start()

    swap_start(3, gh_all.at[0, dp], gh_all.at[0])
    swap_start(4, sums_all.at[dp], sums_all)
    for d, other in enumerate(others):
        pltpu.make_async_remote_copy(
            src_ref=last.at[pl.ds(pl.multiple_of(other * part, part), part)],
            dst_ref=latent.at[me],
            send_sem=lat_send.at[d],
            recv_sem=lat_recv.at[me],
            device_id={"chan": other},
            device_id_type=MESH,
        ).start()
    latent[me] = last[pl.ds(pl.multiple_of(me * part, part), part)]

    @pl.when(top_seg)
    def _():
        spread_inputs()

    far_pass(1)
    swap_finish(2, gh_all.at[1, dp], gh_all.at[1])
    conv_grad(1)
    far_pass(0)
    far_finish(1)
    proj_grad(1)
    far_finish(0)
    proj_grad(0)
    swap_finish(3, gh_all.at[0, dp], gh_all.at[0])
    conv_grad(0)
    swap_finish(4, sums_all.at[dp], sums_all)
    total = sums_all[0]
    for d in range(1, n_dp):
        total = total + sums_all[d]
    sums[...] = total
    for d, other in enumerate(others):
        pltpu.make_async_remote_copy(
            src_ref=last.at[pl.ds(pl.multiple_of(other * part, part), part)],
            dst_ref=latent.at[other],
            send_sem=lat_send.at[d],
            recv_sem=lat_recv.at[other],
            device_id={"chan": other},
            device_id_type=MESH,
        ).wait()

    @pl.when(seg > 0)
    def _():
        relay().wait_send()


def per_device(
    segments, n_chan, n_dp,
    grad_top, inputs_one, conv_one, inputs_two, conv_two,
    proj_weight, conv_weight, norm_gain, norm_bias,
):
    width, pos = conv_one.shape[2:]
    part = pos // n_chan
    chans = proj_weight.shape[3]
    bf = jnp.bfloat16
    f32 = jnp.float32

    top = grad_top.reshape(n_chan, width, part).swapaxes(1, 2)
    w_proj = proj_weight[0]
    proj_shape = (2, width, chans)
    if width % 128:
        w_proj = w_proj.reshape(2, width, n_chan, width).swapaxes(1, 2)
        proj_shape = (2, n_chan, width, width)

    vmem = pl.BlockSpec(memory_space=pltpu.VMEM)
    dma = pltpu.SemaphoreType.DMA
    chips = n_chan // 2
    apart = max(n_dp - 1, 1)
    latent, proj, conv, sums = pl.pallas_call(
        functools.partial(chain_kernel, segments, n_chan, n_dp),
        out_shape=(
            jax.ShapeDtypeStruct((n_chan, part, width), bf),
            jax.ShapeDtypeStruct(proj_shape, f32),
            jax.ShapeDtypeStruct((2, width, 9 * GS), f32),
            jax.ShapeDtypeStruct((2, 2, width), f32),
        ),
        in_specs=[vmem] * 9,
        out_specs=(vmem,) * 4,
        scratch_shapes=[
            pltpu.VMEM((2, n_dp, n_chan, pos, width), bf),
            pltpu.VMEM((2, n_dp, pos, width), bf),
            pltpu.VMEM((n_dp, 2, width, pos), bf),
            pltpu.VMEM((n_dp, 2, width, pos), bf),
            pltpu.VMEM((n_dp, 2, 2, width), f32),
            pltpu.VMEM((pos, width), bf),
            pltpu.VMEM((2, 3, pos + 2 * WW, width // 2), bf),
            pltpu.VMEM((2, n_dp, 3, pos + 2 * WW, width), bf),
            pltpu.VMEM((2, 9, 2, width // 2, width // 2), bf),
            pltpu.VMEM((n_dp, width, pos), bf),
            pltpu.VMEM((width, width), f32),
            pltpu.VMEM((width, width), f32),
            pltpu.VMEM((2, pos, width), f32),
            pltpu.VMEM((2, pos, width), f32),
            pltpu.VMEM((2, 1, width), f32),
            pltpu.VMEM((2, width, pos), bf),
            pltpu.VMEM((2, width, pos), bf),
            pltpu.VMEM((2, n_chan, width, width), bf),
            dma((2, n_chan)),
            dma((2, n_chan)),
            dma,
            dma,
            dma((5, apart)),
            dma((5, n_dp)),
            dma((2, apart, chips)),
            dma((2, n_dp, n_chan)),
            dma((2, apart, chips)),
            dma((n_chan,)),
            dma((n_chan,)),
        ],
        compiler_params=pltpu.CompilerParams(
            collective_id=0, has_side_effects=True, vmem_limit_bytes=60 * 1024 * 1024
        ),
    )(
        top, w_proj, conv_weight[0], norm_gain[0], norm_bias[0],
        conv_one[0, 0], conv_two[0, 0], inputs_one[0, 0], inputs_two[0, 0],
    )

    latent = jnp.swapaxes(latent, 1, 2).reshape(1, 1, chans, part)
    if width % 128:
        proj = proj.swapaxes(1, 2).reshape(2, width, chans)
    return latent, proj[None], conv[None], sums[None, :, 0], sums[None, :, 1]


def solution(mesh):
    return jax.shard_map(
        functools.partial(
            per_device, mesh.shape["segment"], mesh.shape["chan"], mesh.shape["dp"]
        ),
        mesh=mesh,
        in_specs=(
            P("dp", None, "chan"),
            P("segment", "dp", "chan", None),
            P("segment", "dp", "chan", None),
            P("segment", "dp", "chan", None),
            P("segment", "dp", "chan", None),
            P("segment", None, "chan", None),
            P("segment", None, "chan", None),
            P("segment", None, "chan"),
            P("segment", None, "chan"),
        ),
        out_specs=(
            P("segment", "dp", None, "chan"),
            P("segment", None, "chan", None),
            P("segment", None, "chan", None),
            P("segment", None, "chan"),
            P("segment", None, "chan"),
        ),
        check_vma=False,
    )
```

```python
import functools

import jax
import jax.numpy as jnp
from jax import lax
from jax.experimental import pallas as pl
from jax.experimental.pallas import tpu as pltpu
from jax.sharding import PartitionSpec as P

GS = 48
WW = 64
NORM_EPS = 1e-05
CUTS = 4
MESH = pl.DeviceIdType.MESH


def chain_kernel(
    segments, n_chan, n_dp, gtop, wproj, wconv, gain, bias, pre_one, pre_two, in_one, in_two,
    latent, proj, conv, sums,
    g_all, gh_all, act_all, x_all, sums_all, last, taps, x_taps, w_diag, gh_turned, square,
    same, slope, normed, inv_std, act, saved, w_turned,
    send_sems, recv_sems, relay_send, relay_recv, cut_send, cut_recv, dp_send, dp_recv,
    far_send, far_recv, hop_send, lat_send, lat_recv,
):
    seg = lax.axis_index("segment")
    me = lax.axis_index("chan")
    dp = lax.axis_index("dp")
    pos, width = last.shape
    half = width // 2
    part = pos // n_chan
    chips = n_chan // 2
    core = lax.rem(me, 2)
    row = me // 2
    sibling = row * 2 + 1 - core
    peers = [lax.rem(row + d, chips) * 2 + core for d in range(1, chips)]
    others = [lax.rem(me + d, n_chan) for d in range(1, n_chan)]
    replicas = [lax.rem(dp + d, n_dp) for d in range(1, n_dp)]
    top_seg = seg == segments - 1

    barrier = pltpu.get_barrier_semaphore()
    for other in others:
        pl.semaphore_signal(barrier, inc=1, device_id={"chan": other}, device_id_type=MESH)
    for other in replicas:
        pl.semaphore_signal(barrier, inc=1, device_id={"dp": other}, device_id_type=MESH)

    @pl.when(seg > 0)
    def _():
        pl.semaphore_signal(barrier, inc=1, device_id={"segment": seg - 1}, device_id_type=MESH)

    @pl.when(seg < segments - 1)
    def _():
        pl.semaphore_signal(barrier, inc=1, device_id={"segment": seg + 1}, device_id_type=MESH)

    linked = jnp.where(seg > 0, 1, 0) + jnp.where(seg < segments - 1, 1, 0)
    pl.semaphore_wait(barrier, n_chan - 1 + n_dp - 1 + linked)

    def whole(buf):
        return lambda piece: buf.at[piece]

    def strip(buf):
        return lambda piece: buf.at[:, pl.ds(pl.multiple_of(piece * part, part), part)]

    def push(view, which, slot, piece, target):
        return pltpu.make_async_remote_copy(
            src_ref=view(piece),
            dst_ref=view(piece),
            send_sem=send_sems.at[which, slot],
            recv_sem=recv_sems.at[which, piece],
            device_id={"chan": target},
            device_id_type=MESH,
        )

    def gather_start(view, which):
        started = [push(view, which, 1 + d, me, peer) for d, peer in enumerate(peers)]
        started.append(push(view, which, 0, me, sibling))
        for copy in started:
            copy.start()
        return started

    def gather_finish(view, which, started):
        for d, peer in enumerate(peers):
            push(view, which, 1 + d, peer, peer).wait_recv()
            hop = push(view, which, chips + d, peer, sibling)
            hop.start()
            started.append(hop)
        push(view, which, 0, sibling, sibling).wait_recv()
        for d in range(1, chips):
            piece = lax.rem(row + d, chips) * 2 + 1 - core
            push(view, which, 0, piece, sibling).wait_recv()
        for copy in started:
            copy.wait_send()

    def rows(i):
        return pl.ds(i * (pos // CUTS), pos // CUTS)

    def relay(i):
        return pltpu.make_async_remote_copy(
            src_ref=last.at[rows(i)],
            dst_ref=g_all.at[1, dp, me, rows(i)],
            send_sem=relay_send.at[i],
            recv_sem=relay_recv.at[i],
            device_id={"segment": lax.rem(seg + segments - 1, segments)},
            device_id_type=MESH,
        )

    def cut_push(i, slot, piece, target):
        view = g_all.at[1, dp, piece, rows(i)]
        return pltpu.make_async_remote_copy(
            src_ref=view,
            dst_ref=view,
            send_sem=cut_send.at[slot, i],
            recv_sem=cut_recv.at[piece, i],
            device_id={"chan": target},
            device_id_type=MESH,
        )

    def relay_gather():
        started = []
        for i in range(CUTS):
            relay(i).wait_recv()
            copies = [cut_push(i, 1 + d, me, peer) for d, peer in enumerate(peers)]
            copies.append(cut_push(i, 0, me, sibling))
            for copy in copies:
                copy.start()
            started += copies
        for i in range(CUTS):
            for d, peer in enumerate(peers):
                cut_push(i, 1 + d, peer, peer).wait_recv()
                onward = cut_push(i, chips + d, peer, sibling)
                onward.start()
                started.append(onward)
        for i in range(CUTS):
            cut_push(i, 0, sibling, sibling).wait_recv()
            for d in range(1, chips):
                piece = lax.rem(row + d, chips) * 2 + 1 - core
                cut_push(i, 0, piece, sibling).wait_recv()
        for copy in started:
            copy.wait_send()

    def swap(kind, d, src, dst):
        target = replicas[d]
        return pltpu.make_async_remote_copy(
            src_ref=src,
            dst_ref=dst,
            send_sem=dp_send.at[kind, d],
            recv_sem=dp_recv.at[kind, dp],
            device_id={"dp": target},
            device_id_type=MESH,
        )

    def swap_start(kind, src, buf):
        for d in range(n_dp - 1):
            swap(kind, d, src, buf.at[dp]).start()

    def swap_finish(kind, src, buf):
        for d, other in enumerate(replicas):
            pltpu.make_async_remote_copy(
                src_ref=src,
                dst_ref=buf.at[other],
                send_sem=dp_send.at[kind, d],
                recv_sem=dp_recv.at[kind, other],
                device_id={"dp": other},
                device_id_type=MESH,
            ).wait()

    def far(b, d, j, source, piece):
        return pltpu.make_async_remote_copy(
            src_ref=g_all.at[b, source, piece],
            dst_ref=g_all.at[b, source, piece],
            send_sem=far_send.at[b, d, j],
            recv_sem=far_recv.at[b, source, piece],
            device_id={"dp": replicas[d]},
            device_id_type=MESH,
        )

    def hop(b, d, j, source, piece):
        return pltpu.make_async_remote_copy(
            src_ref=g_all.at[b, source, piece],
            dst_ref=g_all.at[b, source, piece],
            send_sem=hop_send.at[b, d, j],
            recv_sem=far_recv.at[b, source, piece],
            device_id={"chan": sibling},
            device_id_type=MESH,
        )

    def far_start(b):
        for d in range(n_dp - 1):
            for j, piece in enumerate([me] + peers):
                far(b, d, j, dp, piece).start()

    def far_pass(b):
        for d, other in enumerate(replicas):
            for j, piece in enumerate([me] + peers):
                far(b, d, j, other, piece).wait_recv()
                hop(b, d, j, other, piece).start()

    def far_finish(b):
        for d, other in enumerate(replicas):
            for j in range(chips):
                piece = lax.rem(row + j, chips) * 2 + 1 - core
                hop(b, d, j, other, piece).wait_recv()
            for j, piece in enumerate([me] + peers):
                far(b, d, j, dp, piece).wait_send()
                hop(b, d, j, other, piece).wait_send()

    column = lax.rem(lax.broadcasted_iota(jnp.int32, (pos, width), 0), WW)

    def side_by_side(values):
        wide = values.astype(jnp.float32)
        ahead = jnp.where(column == WW - 1, 0.0, pltpu.roll(wide, pos - 1, 0))
        behind = jnp.where(column == 0, 0.0, pltpu.roll(wide, 1, 0))
        return ahead.astype(jnp.bfloat16), behind.astype(jnp.bfloat16)

    def spread_taps(b):
        along = lax.broadcasted_iota(jnp.int32, (9 * GS, width), 0)
        within = lax.rem(lax.broadcasted_iota(jnp.int32, (9 * GS, width), 1), GS)
        for k in range(9):
            pick = jnp.where(along == within + k * GS, 1.0, 0.0).astype(jnp.bfloat16)
            tiled = jnp.dot(wconv[b], pick, preferred_element_type=jnp.float32)
            tiled = tiled * same[...]
            for h in range(2):
                side = slice(h * half, (h + 1) * half)
                w_diag[b, k, h] = tiled[side, side].astype(jnp.bfloat16)

    def group_mean(rows):
        return jnp.dot(
            rows, same[...], precision=lax.Precision.HIGHEST, preferred_element_type=jnp.float32
        ) * (1.0 / (GS * pos))

    def column_sum(values):
        return jnp.broadcast_to(jnp.sum(values, axis=0, keepdims=True), (8, width))

    def norm_forward(b):
        pre = (pre_one, pre_two)[b][...].astype(jnp.float32).T
        apart = pre - group_mean(column_sum(pre))[0:1]
        inv = lax.rsqrt(group_mean(column_sum(apart * apart))[0:1] + NORM_EPS)
        xhat = apart * inv
        n = xhat * gain[b:b + 1] + bias[b:b + 1]
        gate = jax.nn.sigmoid(n)
        inv_std[b] = inv
        normed[b] = xhat
        slope[b] = gate * (1.0 + n * (1.0 - gate))
        act[b] = (n * gate).T.astype(jnp.bfloat16)
        for piece in range(n_chan):
            w_turned[b, piece] = piece_of(b, piece).astype(jnp.float32).T.astype(jnp.bfloat16)

    def inputs_start():
        act_all[dp] = act[...]
        x_all[dp] = saved[...]
        swap_start(0, act, act_all)
        swap_start(1, saved, x_all)

    def spread_inputs():
        swap_finish(0, act, act_all)
        swap_finish(1, saved, x_all)
        x_taps[...] = jnp.zeros_like(x_taps)
        for d in range(n_dp):
            for b in range(2):
                values = x_all[d, b].astype(jnp.float32).T.astype(jnp.bfloat16)
                ahead, behind = side_by_side(values)
                x_taps[b, d, 0, WW:WW + pos] = behind
                x_taps[b, d, 1, WW:WW + pos] = values
                x_taps[b, d, 2, WW:WW + pos] = ahead

    def piece_of(b, piece):
        if width % 128 == 0:
            return wproj[b, :, piece * width:(piece + 1) * width]
        return wproj[b, piece]

    def block(b):
        acc = jnp.zeros((pos, width), jnp.float32)
        for piece in range(n_chan):
            acc = acc + lax.dot_general(
                g_all[b, dp, piece], w_turned[b, piece], (((1,), (0,)), ((), ())),
                preferred_element_type=jnp.float32,
            )
        xhat = normed[b]
        gn = acc * slope[b]
        bias_row = jnp.sum(gn, axis=0, keepdims=True)
        gain_row = jnp.sum(gn * xhat, axis=0, keepdims=True)
        sums_all[dp, b, 0:1] = gain_row
        sums_all[dp, b, 1:2] = bias_row
        gains = gain[b:b + 1]
        lane = lax.broadcasted_iota(jnp.int32, (8, width), 0)
        pair = jnp.where(lane == 0, bias_row * gains, jnp.where(lane == 1, gain_row * gains, 0.0))
        means = group_mean(pair)
        gh = inv_std[b] * (gn * gains - means[0:1] - xhat * means[1:2])
        gh = gh.astype(jnp.bfloat16)
        gh_all[b, dp] = gh
        ahead, behind = side_by_side(gh)
        sides = []
        for h in range(2):
            side = slice(h * half, (h + 1) * half)
            for dc, view in enumerate((ahead, gh, behind)):
                taps[h, dc, WW:WW + pos] = view[:, side]
            back = jnp.zeros((pos, half), jnp.float32)
            for dr in range(3):
                start = WW - WW * (dr - 1)
                for dc in range(3):
                    back = back + jnp.dot(
                        taps[h, dc, start:start + pos], w_diag[b, 3 * dr + dc, h],
                        preferred_element_type=jnp.float32,
                    )
            sides.append(back)
        back = jnp.concatenate(sides, axis=1)
        branch = back.astype(jnp.bfloat16).astype(jnp.float32)
        return (g_all[b, dp, me].astype(jnp.float32) + branch).astype(jnp.bfloat16)

    def proj_grad(b):
        for piece in range(n_chan):
            acc = jnp.zeros((width, width), jnp.float32)
            for d in range(n_dp):
                acc = acc + jnp.dot(
                    act_all[d, b], g_all[b, d, piece], preferred_element_type=jnp.float32
                )
            if width % 128 == 0:
                proj[b, :, piece * width:(piece + 1) * width] = acc
            else:
                proj[b, piece] = acc

    def conv_grad(b):
        for d in range(n_dp):
            gh_turned[d] = gh_all[b, d].astype(jnp.float32).T.astype(jnp.bfloat16)
        for dr in range(3):
            start = WW * dr
            for dc in range(3):
                at = (3 * dr + dc) * GS
                acc = jnp.zeros((width, width), jnp.float32)
                for d in range(n_dp):
                    acc = acc + jnp.dot(
                        gh_turned[d], x_taps[b, d, dc, start:start + pos],
                        preferred_element_type=jnp.float32,
                    )
                square[...] = acc
                for q in range(0, width, GS):
                    conv[b, q:q + GS, at:at + GS] = square[q:q + GS, q:q + GS]

    down = lax.broadcasted_iota(jnp.int32, (width, width), 0)
    across = lax.broadcasted_iota(jnp.int32, (width, width), 1)
    same[...] = jnp.where(lax.div(down, GS) == lax.div(across, GS), 1.0, 0.0)
    saved[0] = in_one[...]
    saved[1] = in_two[...]
    taps[...] = jnp.zeros_like(taps)
    entering = g_all.at[1, dp]
    middle = g_all.at[0, dp]

    @pl.when(top_seg)
    def _():
        entering[:, pl.ds(pl.multiple_of(me * part, part), part)] = gtop[...]
        started = gather_start(strip(entering), 1)
        norm_forward(1)
        spread_taps(1)
        gather_finish(strip(entering), 1, started)

    @pl.when(seg < segments - 1)
    def _():
        norm_forward(1)
        norm_forward(0)
        inputs_start()
        spread_taps(1)
        spread_taps(0)
        spread_inputs()
        relay_gather()

    far_start(1)
    middle[me] = block(1)
    started = gather_start(whole(middle), 0)
    swap_start(2, gh_all.at[1, dp], gh_all.at[1])

    @pl.when(top_seg)
    def _():
        norm_forward(0)
        spread_taps(0)
        inputs_start()

    gather_finish(whole(middle), 0, started)
    far_start(0)
    last[...] = block(0)

    @pl.when(seg > 0)
    def _():
        for i in range(CUTS):
            relay(i).start()

    swap_start(3, gh_all.at[0, dp], gh_all.at[0])
    swap_start(4, sums_all.at[dp], sums_all)
    for d, other in enumerate(others):
        pltpu.make_async_remote_copy(
            src_ref=last.at[pl.ds(pl.multiple_of(other * part, part), part)],
            dst_ref=latent.at[me],
            send_sem=lat_send.at[d],
            recv_sem=lat_recv.at[me],
            device_id={"chan": other},
            device_id_type=MESH,
        ).start()
    latent[me] = last[pl.ds(pl.multiple_of(me * part, part), part)]

    @pl.when(top_seg)
    def _():
        spread_inputs()

    far_pass(1)
    swap_finish(2, gh_all.at[1, dp], gh_all.at[1])
    conv_grad(1)
    far_pass(0)
    far_finish(1)
    proj_grad(1)
    far_finish(0)
    proj_grad(0)
    swap_finish(3, gh_all.at[0, dp], gh_all.at[0])
    conv_grad(0)
    swap_finish(4, sums_all.at[dp], sums_all)
    total = sums_all[0]
    for d in range(1, n_dp):
        total = total + sums_all[d]
    sums[...] = total
    for d, other in enumerate(others):
        pltpu.make_async_remote_copy(
            src_ref=last.at[pl.ds(pl.multiple_of(other * part, part), part)],
            dst_ref=latent.at[other],
            send_sem=lat_send.at[d],
            recv_sem=lat_recv.at[other],
            device_id={"chan": other},
            device_id_type=MESH,
        ).wait()

    @pl.when(seg > 0)
    def _():
        for i in range(CUTS):
            relay(i).wait_send()


def per_device(
    segments, n_chan, n_dp,
    grad_top, inputs_one, conv_one, inputs_two, conv_two,
    proj_weight, conv_weight, norm_gain, norm_bias,
):
    width, pos = conv_one.shape[2:]
    part = pos // n_chan
    chans = proj_weight.shape[3]
    bf = jnp.bfloat16
    f32 = jnp.float32

    top = grad_top.reshape(n_chan, width, part).swapaxes(1, 2)
    w_proj = proj_weight[0]
    proj_shape = (2, width, chans)
    if width % 128:
        w_proj = w_proj.reshape(2, width, n_chan, width).swapaxes(1, 2)
        proj_shape = (2, n_chan, width, width)

    vmem = pl.BlockSpec(memory_space=pltpu.VMEM)
    dma = pltpu.SemaphoreType.DMA
    chips = n_chan // 2
    apart = max(n_dp - 1, 1)
    latent, proj, conv, sums = pl.pallas_call(
        functools.partial(chain_kernel, segments, n_chan, n_dp),
        out_shape=(
            jax.ShapeDtypeStruct((n_chan, part, width), bf),
            jax.ShapeDtypeStruct(proj_shape, f32),
            jax.ShapeDtypeStruct((2, width, 9 * GS), f32),
            jax.ShapeDtypeStruct((2, 2, width), f32),
        ),
        in_specs=[vmem] * 9,
        out_specs=(vmem,) * 4,
        scratch_shapes=[
            pltpu.VMEM((2, n_dp, n_chan, pos, width), bf),
            pltpu.VMEM((2, n_dp, pos, width), bf),
            pltpu.VMEM((n_dp, 2, width, pos), bf),
            pltpu.VMEM((n_dp, 2, width, pos), bf),
            pltpu.VMEM((n_dp, 2, 2, width), f32),
            pltpu.VMEM((pos, width), bf),
            pltpu.VMEM((2, 3, pos + 2 * WW, width // 2), bf),
            pltpu.VMEM((2, n_dp, 3, pos + 2 * WW, width), bf),
            pltpu.VMEM((2, 9, 2, width // 2, width // 2), bf),
            pltpu.VMEM((n_dp, width, pos), bf),
            pltpu.VMEM((width, width), f32),
            pltpu.VMEM((width, width), f32),
            pltpu.VMEM((2, pos, width), f32),
            pltpu.VMEM((2, pos, width), f32),
            pltpu.VMEM((2, 1, width), f32),
            pltpu.VMEM((2, width, pos), bf),
            pltpu.VMEM((2, width, pos), bf),
            pltpu.VMEM((2, n_chan, width, width), bf),
            dma((2, n_chan)),
            dma((2, n_chan)),
            dma((CUTS,)),
            dma((CUTS,)),
            dma((n_chan, CUTS)),
            dma((n_chan, CUTS)),
            dma((5, apart)),
            dma((5, n_dp)),
            dma((2, apart, chips)),
            dma((2, n_dp, n_chan)),
            dma((2, apart, chips)),
            dma((n_chan,)),
            dma((n_chan,)),
        ],
        compiler_params=pltpu.CompilerParams(
            collective_id=0, has_side_effects=True, vmem_limit_bytes=60 * 1024 * 1024
        ),
    )(
        top, w_proj, conv_weight[0], norm_gain[0], norm_bias[0],
        conv_one[0, 0], conv_two[0, 0], inputs_one[0, 0], inputs_two[0, 0],
    )

    latent = jnp.swapaxes(latent, 1, 2).reshape(1, 1, chans, part)
    if width % 128:
        proj = proj.swapaxes(1, 2).reshape(2, width, chans)
    return latent, proj[None], conv[None], sums[None, :, 0], sums[None, :, 1]


def solution(mesh):
    return jax.shard_map(
        functools.partial(
            per_device, mesh.shape["segment"], mesh.shape["chan"], mesh.shape["dp"]
        ),
        mesh=mesh,
        in_specs=(
            P("dp", None, "chan"),
            P("segment", "dp", "chan", None),
            P("segment", "dp", "chan", None),
            P("segment", "dp", "chan", None),
            P("segment", "dp", "chan", None),
            P("segment", None, "chan", None),
            P("segment", None, "chan", None),
            P("segment", None, "chan"),
            P("segment", None, "chan"),
        ),
        out_specs=(
            P("segment", "dp", None, "chan"),
            P("segment", None, "chan", None),
            P("segment", None, "chan", None),
            P("segment", None, "chan"),
            P("segment", None, "chan"),
        ),
        check_vma=False,
    )
```
